256 devices in a mesh: rows: 64 (over y, x, z_lo, core), cols: 4 (over z_hi).
Axes of the slice: x: 4, y: 4, z: 8 (z_hi: 4, z_lo: 2; z = z_hi * 2 + z_lo), core: 2. Of those that a mesh axis runs over, the one named last changes fastest.
Arguments:
- noise: bfloat16 [32768, 4096], P('rows'), may hold values from -12 to 12
- data: bfloat16 [4096, 4096], P('cols', 'rows'), may hold values from -12 to 12
Outputs:
- targets: bfloat16 [32768, 4096], P('rows', 'cols')
- row_potential: float32 [32768], P('rows')
- col_potential: float32 [4096], P('cols')
The draws below stay inside these ranges and needn't reach their ends.
All inputs are finite; a program needn't handle non-finite values.
Results may differ from the reference program's by a relative error of at most 0.012.
Values may be sent and summed in bfloat16 or wider, within the bound.
A program may use at most 64 MiB of HBM per device.

```python
import math
import jax
import jax.numpy as jnp
from jax import lax

WIDTH = 4096
ITERS = 4
COL_DEV = 1024
NOISE_ROWS = 32768
DATA_ROWS = 4096
N_COLS = 4


def scaled_rows(key, count, low, high):
    return jnp.exp(jax.random.uniform(key, (count, 1), jnp.float32, math.log(low), math.log(high)))


def draw_noise(key, part):
    key = jax.random.fold_in(key, 11)
    key_scale, key_jitter, key_factor = jax.random.split(key, 3)
    shared = 16
    row_scale = scaled_rows(key_scale, NOISE_ROWS, 0.7, 1.4)
    factors = jax.random.normal(key_factor, (NOISE_ROWS, 1, shared), jnp.float32)
    jitter = jax.random.normal(key_jitter, (NOISE_ROWS, WIDTH // shared, shared), jnp.float32)
    values = (0.7 * factors + jitter).reshape(NOISE_ROWS, WIDTH)
    return jnp.clip(row_scale * values, -12.0, 12.0).astype(jnp.bfloat16)


def draw_data(key, part):
    key = jax.random.fold_in(key, 12)
    key_scale, key_jitter, key_factor = jax.random.split(key, 3)
    shared = 16
    row_scale = scaled_rows(key_scale, DATA_ROWS, 0.7, 1.4)
    factors = jax.random.normal(key_factor, (DATA_ROWS, 1, shared), jnp.float32)
    jitter = jax.random.normal(key_jitter, (DATA_ROWS, WIDTH // shared, shared), jnp.float32)
    values = (0.7 * factors + jitter).reshape(DATA_ROWS, WIDTH)
    return jnp.clip(row_scale * values, -12.0, 12.0).astype(jnp.bfloat16)


def setup_inputs(seed: int = 0) -> dict:
    key_of = jax.random.split(jax.random.key(seed), 3)
    return {
        "noise": draw_noise(jax.random.fold_in(key_of[2], 71), 0),
        "data": draw_data(jax.random.fold_in(key_of[2], 71), 0),
    }


EPSILON = 0.05


def log_sum_exp(values, axis):
    top = jnp.max(values, axis=axis, keepdims=True)
    total = jnp.sum(jnp.exp(values - top), axis=axis)
    return jnp.squeeze(top, axis) + jnp.log(total)


def reference(noise, data):
    noise_wide = noise.astype(jnp.float32)
    data_wide = data.astype(jnp.float32)
    gram = jnp.dot(noise_wide, data_wide.T, preferred_element_type=jnp.float32, precision=lax.Precision.HIGHEST)
    noise_sq = jnp.sum(noise_wide * noise_wide, axis=1)
    data_sq = jnp.sum(data_wide * data_wide, axis=1)
    cost = (noise_sq[:, None] + data_sq[None, :] - 2.0 * gram) / WIDTH
    log_rows = -math.log(NOISE_ROWS)
    log_cols = -math.log(DATA_ROWS)
    col_potential = jnp.zeros((DATA_ROWS,), jnp.float32)
    row_potential = jnp.zeros((NOISE_ROWS,), jnp.float32)
    for step in range(ITERS):
        row_potential = EPSILON * (log_rows - log_sum_exp((col_potential[None, :] - cost) / EPSILON, 1))
        col_potential = EPSILON * (log_cols - log_sum_exp((row_potential[:, None] - cost) / EPSILON, 0))
    logits = (col_potential[None, :] - cost) / EPSILON
    weights = jnp.exp(logits - log_sum_exp(logits, 1)[:, None]).astype(jnp.bfloat16)
    targets = jnp.zeros((NOISE_ROWS, WIDTH), jnp.float32)
    for block in range(N_COLS):
        block_weights = weights[:, block * COL_DEV:(block + 1) * COL_DEV].astype(jnp.float32)
        block_data = data_wide[block * COL_DEV:(block + 1) * COL_DEV]
        product = jnp.dot(block_weights, block_data, preferred_element_type=jnp.float32, precision=lax.Precision.HIGHEST)
        rounded = lax.optimization_barrier(product.astype(jnp.bfloat16))
        targets = targets + rounded.astype(jnp.float32)
    return targets.astype(jnp.bfloat16), row_potential, col_potential
```

```python
import functools
import math

import jax
import jax.numpy as jnp
from jax import lax
from jax.experimental import pallas as pl
from jax.experimental.pallas import tpu as pltpu
from jax.sharding import PartitionSpec as P

ITERS = 4
EPSILON = 0.05
SCALE_BITS = 64.0
SCALE = 2.0**64
MESH = pl.DeviceIdType.MESH
F32 = jnp.float32
BF16 = jnp.bfloat16


def kernel(
    noise_ref, data_ref, out_ref, row_ref, col_ref,
    whole, scores, mass, weights, rmsg, rbuf, cmsg, cbuf,
    gsend, grecv, bsend, brecv, rsend, rrecv, csend, crecv,
):
    rows_total = 32768
    cols_total = 4096
    width = 4096
    to_log2 = 1.0 / (EPSILON * math.log(2.0))
    me = lax.axis_index("rows")
    zh = lax.axis_index("cols")
    y, x, zl, core = me // 16, (me // 4) % 4, (me // 2) % 2, me % 2

    def index(yy, xx, ll):
        return ((((yy + 4) % 4) * 4 + (xx + 4) % 4) * 2 + ll) * 2 + core

    barrier = pltpu.get_barrier_semaphore()

    def greet(o, carry):
        pl.semaphore_signal(barrier, inc=1, device_id=((me + o) % 64, zh), device_id_type=MESH)
        return carry

    lax.fori_loop(1, 64, greet, 0)
    for o in range(1, 4):
        pl.semaphore_signal(barrier, inc=1, device_id=(me, (zh + o) % 4), device_id_type=MESH)

    eye = (
        lax.broadcasted_iota(jnp.int32, (64, 64), 0) == lax.broadcasted_iota(jnp.int32, (64, 64), 1)
    ).astype(F32).astype(BF16)
    whole[me] = lax.dot_general(
        eye, data_ref[...], (((1,), (1,)), ((), ())), preferred_element_type=F32
    ).astype(BF16)
    pl.semaphore_wait(barrier, 66)

    sends = []

    def move(t, slot, target, half=None):
        ref = whole.at[slot] if half is None else whole.at[slot, pl.ds(half * 32, 32)]
        copy = pltpu.make_async_remote_copy(
            src_ref=ref, dst_ref=ref, send_sem=gsend.at[t], recv_sem=grecv.at[t],
            device_id=(target, zh), device_id_type=MESH,
        )
        copy.start()
        sends.append(copy)

    def arrived(t, slot, half=None):
        ref = whole.at[slot] if half is None else whole.at[slot, pl.ds(half * 32, 32)]
        pltpu.make_async_remote_copy(
            src_ref=ref, dst_ref=ref, send_sem=gsend.at[t], recv_sem=grecv.at[t],
            device_id=(me, zh), device_id_type=MESH,
        ).wait_recv()

    sibling = me + 1 - 2 * core
    shared = []

    def share(slot):
        t = len(shared)
        copy = pltpu.make_async_remote_copy(
            src_ref=whole.at[slot], dst_ref=whole.at[slot], send_sem=bsend.at[t],
            recv_sem=brecv.at[t], device_id=(sibling, zh), device_id_type=MESH,
        )
        copy.start()
        shared.append((copy, slot + 1 - 2 * core))

    move(0, me, index(y, x, 1 - zl))
    share(me)
    arrived(0, index(y, x, 1 - zl))
    share(index(y, x, 1 - zl))

    def at(part, da, db):
        return index(y + db, x + da, 0) if part == 0 else index(y + da, x + db, 1)

    def near(part, da, db):
        return index(y + db, x + da, zl) if part == 0 else index(y + da, x + db, zl)

    base = (1, 25)
    second = ((0, 0), (-1, 3), (1, 6), (2, 9))
    for part in (0, 1):
        b = base[part]
        move(b + 0, at(part, 0, 0), near(part, 1, 0))
        move(b + 1, at(part, 0, 0), near(part, -1, 0))

    def along_second(part, da, n):
        b = base[part] + 4 + 5 * n
        move(b + 0, at(part, da, 0), near(part, 0, 1))
        move(b + 1, at(part, da, 0), near(part, 0, -1))

    for part in (0, 1):
        along_second(part, 0, 0)
    for part in (0, 1):
        b = base[part]
        arrived(b + 0, at(part, -1, 0))
        move(b + 2, at(part, -1, 0), near(part, 1, 0), 0)
        arrived(b + 1, at(part, 1, 0))
        move(b + 3, at(part, 1, 0), near(part, -1, 0), 1)
    for part in (0, 1):
        along_second(part, -1, 1)
        share(at(part, -1, 0))
        along_second(part, 1, 2)
        share(at(part, 1, 0))

    def relay(part, da, n, up):
        b = base[part] + 4 + 5 * n
        arrived(b + 0, at(part, da, -1))
        if up:
            move(b + 2, at(part, da, -1), near(part, 0, 1))
        share(at(part, da, -1))
        arrived(b + 1, at(part, da, 1))
        if not up:
            move(b + 2, at(part, da, 1), near(part, 0, -1))
        share(at(part, da, 1))

    for part in (0, 1):
        relay(part, 0, 0, True)
    for part in (0, 1):
        b = base[part]
        arrived(b + 2, at(part, 2, 0), 0)
        arrived(b + 3, at(part, 2, 0), 1)
        along_second(part, 2, 3)
        share(at(part, 2, 0))
    for part in (0, 1):
        relay(part, -1, 1, False)
        relay(part, 1, 2, True)
    for part in (0, 1):
        relay(part, 2, 3, False)
    for n, da in enumerate((0, -1, 1, 2)):
        for part in (0, 1):
            b = base[part] + 4 + 5 * n
            arrived(b + 2, at(part, da, 2))
            share(at(part, da, 2))
    for copy in sends:
        copy.wait_send()
    for copy, slot in shared:
        copy.wait_send()
        copy.wait_recv()

    factor = 2.0 * to_log2 / width

    @pl.loop(0, 4)
    def _(n):
        cols = pl.ds(pl.multiple_of(n * 256, 256), 256)
        right = whole[:, :, cols].reshape(4096, 256)
        scores[:, cols] = factor * jnp.dot(noise_ref[...], right, preferred_element_type=F32)

    def square_cols(i, acc):
        v = whole[i].astype(F32)
        v = v * v
        return acc + jnp.sum(v.reshape(8, 8, 1024), axis=0)

    data_sq = jnp.sum(lax.fori_loop(0, 64, square_cols, jnp.zeros((8, 1024), F32)), axis=0, keepdims=True)

    diagonal = lax.broadcasted_iota(jnp.int32, (128, 128), 0) == lax.broadcasted_iota(jnp.int32, (128, 128), 1)

    def compact(column):
        parts = [
            jnp.sum(jnp.where(diagonal, column[i * 128:(i + 1) * 128], 0.0), axis=0, keepdims=True)
            for i in range(4)
        ]
        return jnp.concatenate(parts + parts, axis=0)

    def spread(packed):
        parts = [
            jnp.sum(jnp.where(diagonal, packed[i:i + 1], 0.0), axis=1, keepdims=True)
            for i in range(4)
        ]
        return jnp.concatenate(parts, axis=0)

    def fold(line):
        return jnp.concatenate([line[:, i * 128:(i + 1) * 128] for i in range(8)], axis=0)

    def unfold(packed):
        return jnp.concatenate([packed[i:i + 1] for i in range(8)], axis=1)

    def exchange_rows(e, packed):
        rmsg[e] = packed
        for o in range(1, 4):
            pltpu.make_async_remote_copy(
                src_ref=rmsg.at[e], dst_ref=rbuf.at[e, o - 1], send_sem=rsend.at[e, o - 1],
                recv_sem=rrecv.at[e, o - 1], device_id=(me, (zh + o) % 4), device_id_type=MESH,
            ).start()
        for o in range(1, 4):
            pltpu.make_async_remote_copy(
                src_ref=rmsg.at[e], dst_ref=rbuf.at[e, o - 1], send_sem=rsend.at[e, o - 1],
                recv_sem=rrecv.at[e, o - 1], device_id=(me, (zh + o) % 4), device_id_type=MESH,
            ).wait()
        return rbuf[e]

    def exchange_cols(e, packed):
        cmsg[e] = packed

        def start(o, carry):
            pltpu.make_async_remote_copy(
                src_ref=cmsg.at[e], dst_ref=cbuf.at[e, o - 1], send_sem=csend.at[e],
                recv_sem=crecv.at[e], device_id=((me + o) % 64, zh), device_id_type=MESH,
            ).start()
            return carry

        lax.fori_loop(1, 64, start, 0)
        everything = pltpu.make_async_remote_copy(
            src_ref=cbuf.at[e], dst_ref=cbuf.at[e], send_sem=csend.at[e],
            recv_sem=crecv.at[e], device_id=(sibling, zh), device_id_type=MESH,
        )
        everything.wait_recv()
        everything.wait_send()
        return cbuf[e]

    def combine(own, others):
        top = jnp.maximum(own, jnp.max(others, axis=0))
        total = jnp.exp2(own - top) + jnp.sum(jnp.exp2(others - top[None]), axis=0)
        return top + jnp.log2(total)

    log_rows = -math.log2(rows_total)
    log_cols = -math.log2(cols_total)

    start_cols = data_sq * (-to_log2 / width)
    logits = scores[...] + start_cols
    top = jnp.max(logits, axis=1, keepdims=True)
    own = compact(top + jnp.log2(jnp.sum(jnp.exp2(logits - top), axis=1, keepdims=True)))
    row_pot = log_rows - combine(own, exchange_rows(0, own))
    logits = scores[...] + spread(row_pot)
    top = jnp.max(logits, axis=0, keepdims=True)
    own = fold(top + jnp.log2(jnp.sum(jnp.exp2(logits - top), axis=0, keepdims=True)))
    col_pot = log_cols - combine(own, exchange_cols(0, own))
    mass[...] = jnp.exp2(scores[...] + (spread(row_pot) + SCALE_BITS) + unfold(col_pot))

    right_scale = jnp.ones((8, 128), F32)
    for e in range(1, ITERS):
        own = compact(jnp.sum(mass[...] * unfold(right_scale), axis=1, keepdims=True))
        total = own + jnp.sum(exchange_rows(e, own), axis=0)
        left_scale = (SCALE / rows_total) / total
        own = fold(jnp.sum(mass[...] * spread(left_scale), axis=0, keepdims=True))
        total = own + jnp.sum(exchange_cols(e, own), axis=0)
        right_scale = (SCALE / cols_total) / total

    row_log = row_pot + jnp.log2(left_scale)
    col_log = col_pot + jnp.log2(right_scale)

    v = noise_ref[...].astype(F32)
    noise_sq = compact(jnp.sum(v * v, axis=1, keepdims=True))
    row_ref[...] = row_log * (1.0 / to_log2) + noise_sq * (1.0 / width)
    col_ref[...] = col_log * (1.0 / to_log2) + fold(data_sq) * (1.0 / width)

    plan = mass[...] * unfold(right_scale)
    own = compact(jnp.sum(plan, axis=1, keepdims=True))
    total = own + jnp.sum(exchange_rows(ITERS, own), axis=0)
    weights[...] = (plan * spread(1.0 / total)).astype(BF16)

    @pl.loop(0, 8)
    def _(n):
        right = whole[pl.ds(n * 8, 8)].reshape(512, 1024)
        cols = pl.ds(pl.multiple_of(n * 512, 512), 512)
        out_ref[:, cols] = lax.dot_general(
            weights[...], right, (((1,), (1,)), ((), ())), preferred_element_type=F32
        ).astype(BF16)


def per_device(noise, data):
    vmem = pl.BlockSpec(memory_space=pltpu.VMEM)
    dma = pltpu.SemaphoreType.DMA
    partial, row_pot, col_pot = pl.pallas_call(
        kernel,
        out_shape=(
            jax.ShapeDtypeStruct((512, 4096), BF16),
            jax.ShapeDtypeStruct((8, 128), F32),
            jax.ShapeDtypeStruct((8, 128), F32),
        ),
        in_specs=[vmem, vmem],
        out_specs=(vmem, vmem, vmem),
        scratch_shapes=[
            pltpu.VMEM((64, 64, 1024), BF16),
            pltpu.VMEM((512, 1024), F32),
            pltpu.VMEM((512, 1024), F32),
            pltpu.VMEM((512, 1024), BF16),
            pltpu.VMEM((ITERS + 1, 8, 128), F32),
            pltpu.VMEM((ITERS + 1, 3, 8, 128), F32),
            pltpu.VMEM((ITERS, 8, 128), F32),
            pltpu.VMEM((ITERS, 63, 8, 128), F32),
            dma((49,)),
            dma((49,)),
            dma((32,)),
            dma((32,)),
            dma((ITERS + 1, 3)),
            dma((ITERS + 1, 3)),
            dma((ITERS,)),
            dma((ITERS,)),
        ],
        compiler_params=pltpu.CompilerParams(
            collective_id=0, has_side_effects=True, vmem_limit_bytes=56 * 2**20
        ),
        cost_estimate=pl.CostEstimate(flops=9 * 10**9, bytes_accessed=9 * 2**20, transcendentals=3 * 10**6),
    )(noise, data)
    targets = lax.psum_scatter(partial, "cols", scatter_dimension=1, tiled=True)
    return targets, row_pot[:4].reshape(512), col_pot.reshape(1024)


def solution(mesh):
    in_specs = (P("rows", None), P("cols", "rows"))
    out_specs = (P("rows", "cols"), P("rows"), P("cols"))
    return jax.shard_map(
        per_device, mesh=mesh, in_specs=in_specs, out_specs=out_specs, check_vma=False
    )
```

```python
import functools
import math

import jax
import jax.numpy as jnp
from jax import lax
from jax.experimental import pallas as pl
from jax.experimental.pallas import tpu as pltpu
from jax.sharding import PartitionSpec as P

ITERS = 4
EPSILON = 0.05
SCALE_BITS = 64.0
SCALE = 2.0**64
MESH = pl.DeviceIdType.MESH
F32 = jnp.float32
BF16 = jnp.bfloat16


def kernel(
    noise_hbm, data_ref, out_ref, row_ref, col_ref,
    noise_ref, whole_a, whole_b, scores, mass, plan_ref, part_ref, got_ref, own_ref,
    rmsg, rbuf, cmsg, cbuf, pmsg, pbuf,
    nsem, zsend, zrecv, asems, bsems, rsend, rrecv, csend, crecv, psend, precv, tsend, trecv,
):
    rows_total = 32768
    cols_total = 4096
    width = 4096
    to_log2 = 1.0 / (EPSILON * math.log(2.0))
    factor = 2.0 * to_log2 / width
    me = lax.axis_index("rows")
    zh = lax.axis_index("cols")
    y, x, zl, core = me // 16, (me // 4) % 4, (me // 2) % 2, me % 2
    sibling = me + 1 - 2 * core

    def index(yy, xx, ll):
        return ((((yy + 4) % 4) * 4 + (xx + 4) % 4) * 2 + ll) * 2 + core

    load = pltpu.make_async_copy(noise_hbm, noise_ref, nsem)
    load.start()

    barrier = pltpu.get_barrier_semaphore()

    def greet(o, carry):
        pl.semaphore_signal(barrier, inc=1, device_id=((me + o) % 64, zh), device_id_type=MESH)
        return carry

    lax.fori_loop(1, 64, greet, 0)
    for o in range(1, 4):
        pl.semaphore_signal(barrier, inc=1, device_id=(me, (zh + o) % 4), device_id_type=MESH)
    whole_a[me] = data_ref[...]
    pl.semaphore_wait(barrier, 66)

    def at(part, da, db):
        return index(y + db, x + da, 0) if part == 0 else index(y + da, x + db, 1)

    def near(part, da, db):
        return index(y + db, x + da, zl) if part == 0 else index(y + da, x + db, zl)

    base = (1, 25)
    turns = (0, -1, 1, 2)

    class Gather:
        def __init__(self, whole, sems):
            self.whole = whole
            self.gsend, self.grecv, self.bsend, self.brecv = sems
            self.sent = []
            self.shared = 0
            self.of_turn = {n: [] for n in range(4)}

        def remote(self, slot, half, send, recv, target):
            ref = self.whole.at[slot] if half is None else self.whole.at[slot, pl.ds(half * 32, 32)]
            return pltpu.make_async_remote_copy(
                src_ref=ref, dst_ref=ref, send_sem=send, recv_sem=recv,
                device_id=(target, zh), device_id_type=MESH,
            )

        def move(self, t, slot, target, half=None):
            copy = self.remote(slot, half, self.gsend.at[t], self.grecv.at[t], target)
            copy.start()
            self.sent.append(copy)

        def arrived(self, t, slot, half=None):
            self.remote(slot, half, self.gsend.at[t], self.grecv.at[t], sibling).wait_recv()

        def share(self, slot, n):
            t = self.shared
            self.shared += 1
            copy = self.remote(slot, None, self.bsend.at[t], self.brecv.at[t], sibling)
            copy.start()
            self.sent.append(copy)
            theirs = slot + 1 - 2 * core
            self.of_turn[n].append(self.remote(theirs, None, self.bsend.at[t], self.brecv.at[t], sibling))

        def begin(self):
            self.move(0, me, index(y, x, 1 - zl))
            self.share(me, 0)

        def first(self):
            self.arrived(0, index(y, x, 1 - zl))
            for part in (0, 1):
                b = base[part]
                self.move(b + 0, at(part, 0, 0), near(part, 1, 0))
                self.move(b + 1, at(part, 0, 0), near(part, -1, 0))
            self.share(index(y, x, 1 - zl), 0)

        def second(self, n):
            for part in (0, 1):
                b = base[part] + 4 + 5 * n
                self.move(b + 0, at(part, turns[n], 0), near(part, 0, 1))
                self.move(b + 1, at(part, turns[n], 0), near(part, 0, -1))

        def halves(self):
            for part in (0, 1):
                b = base[part]
                self.arrived(b + 0, at(part, -1, 0))
                self.move(b + 2, at(part, -1, 0), near(part, 1, 0), 0)
                self.arrived(b + 1, at(part, 1, 0))
                self.move(b + 3, at(part, 1, 0), near(part, -1, 0), 1)

        def share_first(self):
            for part in (0, 1):
                self.share(at(part, -1, 0), 1)
                self.share(at(part, 1, 0), 2)

        def opposite(self):
            for part in (0, 1):
                b = base[part]
                self.arrived(b + 2, at(part, 2, 0), 0)
                self.arrived(b + 3, at(part, 2, 0), 1)
                self.share(at(part, 2, 0), 3)

        def relay(self, n, up):
            for part in (0, 1):
                b = base[part] + 4 + 5 * n
                self.arrived(b + 0, at(part, turns[n], -1))
                if up:
                    self.move(b + 2, at(part, turns[n], -1), near(part, 0, 1))
                self.share(at(part, turns[n], -1), n)
                self.arrived(b + 1, at(part, turns[n], 1))
                if not up:
                    self.move(b + 2, at(part, turns[n], 1), near(part, 0, -1))
                self.share(at(part, turns[n], 1), n)

        def last(self, n):
            for part in (0, 1):
                self.arrived(base[part] + 4 + 5 * n + 2, at(part, turns[n], 2))
                self.share(at(part, turns[n], 2), n)

        def turn_done(self, n):
            for copy in self.of_turn[n]:
                copy.wait_recv()

        def done(self):
            for copy in self.sent:
                copy.wait_send()

    def add_gram(whole, n, keep):
        for part in (0, 1):
            firsts = [
                (((i * 4 + (x + turns[n] + 4) % 4) * 2 + part) * 2) if part == 0
                else (((((y + turns[n] + 4) % 4) * 4 + i) * 2 + part) * 2)
                for i in range(4)
            ]
            left = jnp.concatenate(
                [noise_ref[:, pl.ds(pl.multiple_of(f * 64, 128), 128)] for f in firsts], axis=1
            )
            for c in range(4):
                cols = pl.ds(c * 256, 256)
                right = jnp.concatenate(
                    [whole[pl.ds(f, 2), :, cols].reshape(128, 256) for f in firsts], axis=0
                )
                value = factor * jnp.dot(left, right, preferred_element_type=F32)
                scores[:, cols] = value if n == 0 and part == 0 else scores[:, cols] + value

    first_block = Gather(whole_a, [asems.at[i] for i in range(4)])
    other_block = Gather(whole_b, [bsems.at[i] for i in range(4)])

    first_block.begin()
    across = pltpu.make_async_remote_copy(
        src_ref=whole_a.at[me], dst_ref=whole_b.at[me], send_sem=zsend, recv_sem=zrecv,
        device_id=(me, (zh + 2) % 4), device_id_type=MESH,
    )
    first_block.first()
    across.start()
    first_block.second(0)
    first_block.halves()
    first_block.second(1)
    first_block.second(2)
    first_block.share_first()
    first_block.relay(0, True)
    first_block.opposite()
    first_block.second(3)
    first_block.relay(1, False)
    first_block.relay(2, True)
    first_block.last(0)
    first_block.relay(3, False)
    load.wait()
    first_block.turn_done(0)
    add_gram(whole_a, 0, False)
    for n in (1, 2, 3):
        first_block.last(n)
        first_block.turn_done(n)
        add_gram(whole_a, n, False)

    def square_cols(i, acc):
        v = whole_a[i].astype(F32)
        v = v * v
        return acc + jnp.sum(v.reshape(8, 8, 1024), axis=0)

    data_sq = jnp.sum(lax.fori_loop(0, 64, square_cols, jnp.zeros((8, 1024), F32)), axis=0, keepdims=True)
    diagonal = lax.broadcasted_iota(jnp.int32, (128, 128), 0) == lax.broadcasted_iota(jnp.int32, (128, 128), 1)

    def compact(column):
        parts = [
            jnp.sum(jnp.where(diagonal, column[i * 128:(i + 1) * 128], 0.0), axis=0, keepdims=True)
            for i in range(4)
        ]
        return jnp.concatenate(parts + parts, axis=0)

    def spread(packed):
        parts = [
            jnp.sum(jnp.where(diagonal, packed[i:i + 1], 0.0), axis=1, keepdims=True)
            for i in range(4)
        ]
        return jnp.concatenate(parts, axis=0)

    def fold(line):
        return jnp.concatenate([line[:, i * 128:(i + 1) * 128] for i in range(8)], axis=0)

    def unfold(packed):
        return jnp.concatenate([packed[i:i + 1] for i in range(8)], axis=1)

    def exchange_rows(e, packed, between):
        rmsg[e] = packed
        copies = [
            pltpu.make_async_remote_copy(
                src_ref=rmsg.at[e], dst_ref=rbuf.at[e, o - 1], send_sem=rsend.at[e, o - 1],
                recv_sem=rrecv.at[e, o - 1], device_id=(me, (zh + o) % 4), device_id_type=MESH,
            )
            for o in range(1, 4)
        ]
        for copy in copies:
            copy.start()
        between()
        for copy in copies:
            copy.wait()
        return rbuf[e]

    def exchange_cols(e, packed, between):
        cmsg[e] = packed

        def start(o, carry):
            pltpu.make_async_remote_copy(
                src_ref=cmsg.at[e], dst_ref=cbuf.at[e, o - 1], send_sem=csend.at[e],
                recv_sem=crecv.at[e], device_id=((me + o) % 64, zh), device_id_type=MESH,
            ).start()
            return carry

        lax.fori_loop(1, 64, start, 0)
        between()
        everything = pltpu.make_async_remote_copy(
            src_ref=cbuf.at[e], dst_ref=cbuf.at[e], send_sem=csend.at[e],
            recv_sem=crecv.at[e], device_id=(sibling, zh), device_id_type=MESH,
        )
        everything.wait_recv()
        everything.wait_send()
        return cbuf[e]

    def step_r1():
        across.wait()
        other_block.begin()

    def step_c1():
        other_block.first()

    def step_r2():
        other_block.halves()
        other_block.second(0)
        other_block.share_first()

    def step_c2():
        other_block.second(1)
        other_block.opposite()

    def step_r3():
        other_block.second(2)

    def step_c3():
        other_block.relay(0, True)
        other_block.second(3)

    def step_r4():
        other_block.relay(1, False)
        other_block.relay(2, True)
        other_block.last(0)

    def step_c4():
        other_block.relay(3, False)

    row_steps = (step_r1, step_r2, step_r3, step_r4)
    col_steps = (step_c1, step_c2, step_c3, step_c4)

    def combine(own, others):
        top = jnp.maximum(own, jnp.max(others, axis=0))
        total = jnp.exp2(own - top) + jnp.sum(jnp.exp2(others - top[None]), axis=0)
        return top + jnp.log2(total)

    log_rows = -math.log2(rows_total)
    log_cols = -math.log2(cols_total)

    start_cols = data_sq * (-to_log2 / width)
    logits = scores[...] + start_cols
    top = jnp.max(logits, axis=1, keepdims=True)
    own = compact(top + jnp.log2(jnp.sum(jnp.exp2(logits - top), axis=1, keepdims=True)))
    row_pot = log_rows - combine(own, exchange_rows(0, own, row_steps[0]))
    logits = scores[...] + spread(row_pot)
    top = jnp.max(logits, axis=0, keepdims=True)
    own = fold(top + jnp.log2(jnp.sum(jnp.exp2(logits - top), axis=0, keepdims=True)))
    col_pot = log_cols - combine(own, exchange_cols(0, own, col_steps[0]))
    mass[...] = jnp.exp2(scores[...] + (spread(row_pot) + SCALE_BITS) + unfold(col_pot))

    right_scale = jnp.ones((8, 128), F32)
    for e in range(1, ITERS):
        own = compact(jnp.sum(mass[...] * unfold(right_scale), axis=1, keepdims=True))
        total = own + jnp.sum(exchange_rows(e, own, row_steps[e]), axis=0)
        left_scale = (SCALE / rows_total) / total
        own = fold(jnp.sum(mass[...] * spread(left_scale), axis=0, keepdims=True))
        total = own + jnp.sum(exchange_cols(e, own, col_steps[e]), axis=0)
        right_scale = (SCALE / cols_total) / total

    row_log = row_pot + jnp.log2(left_scale)
    col_log = col_pot + jnp.log2(right_scale)

    pmsg[0] = col_log
    swap = pltpu.make_async_remote_copy(
        src_ref=pmsg.at[0], dst_ref=pbuf.at[0], send_sem=psend.at[0], recv_sem=precv.at[0],
        device_id=(me, (zh + 2) % 4), device_id_type=MESH,
    )
    swap.start()
    row_bits = spread(row_log)
    plan = jnp.exp2(scores[...] + row_bits + unfold(col_log))
    plan_ref[:, :1024] = plan.astype(BF16)
    sums = jnp.sum(plan, axis=1, keepdims=True)

    other_block.turn_done(0)
    add_gram(whole_b, 0, False)
    for n in (1, 2, 3):
        other_block.last(n)
        other_block.turn_done(n)
        add_gram(whole_b, n, False)
    swap.wait()
    plan = jnp.exp2(scores[...] + row_bits + unfold(pbuf[0]))
    plan_ref[:, 1024:] = plan.astype(BF16)
    sums = compact(sums + jnp.sum(plan, axis=1, keepdims=True))
    pmsg[1] = sums
    tell = pltpu.make_async_remote_copy(
        src_ref=pmsg.at[1], dst_ref=pbuf.at[1], send_sem=psend.at[1], recv_sem=precv.at[1],
        device_id=(me, (zh + 1) % 4), device_id_type=MESH,
    )
    tell.start()

    def product(rows, q, c):
        total = None
        for half, whole in ((0, whole_a), (1, whole_b)):
            right = whole[pl.ds(q * 16 + c * 4, 4)].reshape(256, 1024)
            value = lax.dot_general(
                plan_ref[rows, pl.ds(half * 1024, 1024)], right, (((1,), (1,)), ((), ())),
                preferred_element_type=F32,
            )
            total = value if total is None else total + value
        return total

    hand = []
    for c in range(4):
        for d, step in ((0, 1), (1, 3)):
            q = (zh + step) % 4
            part_ref[d, c] = product(pl.ds(d * 256, 256), q, c).astype(BF16)
            copy = pltpu.make_async_remote_copy(
                src_ref=part_ref.at[d, c], dst_ref=got_ref.at[d, c], send_sem=tsend.at[d, c],
                recv_sem=trecv.at[d, c], device_id=(me, q), device_id_type=MESH,
            )
            copy.start()
            hand.append(copy)
    for c in range(4):
        own_ref[:, pl.ds(c * 256, 256)] = product(pl.ds(0, 512), zh, c)

    v = noise_ref[...].astype(F32)
    noise_sq = compact(jnp.sum(v * v, axis=1, keepdims=True))
    row_ref[...] = row_log * (1.0 / to_log2) + noise_sq * (1.0 / width)
    col_ref[...] = col_log * (1.0 / to_log2) + fold(data_sq) * (1.0 / width)

    tell.wait()
    inverse = spread(1.0 / (sums + pbuf[1]))
    for c in range(4):
        for d in (0, 1):
            hand[c * 2 + d].wait_recv()
            rows, cols = pl.ds(d * 256, 256), pl.ds(c * 256, 256)
            value = own_ref[rows, cols] + got_ref[d, c].astype(F32)
            out_ref[rows, cols] = (value * inverse[d * 256:(d + 1) * 256]).astype(BF16)
    for copy in hand:
        copy.wait_send()
    first_block.done()
    other_block.done()


def per_device(noise, data):
    vmem = pl.BlockSpec(memory_space=pltpu.VMEM)
    dma = pltpu.SemaphoreType.DMA
    targets, row_pot, col_pot = pl.pallas_call(
        kernel,
        out_shape=(
            jax.ShapeDtypeStruct((512, 1024), BF16),
            jax.ShapeDtypeStruct((8, 128), F32),
            jax.ShapeDtypeStruct((8, 128), F32),
        ),
        in_specs=[pl.BlockSpec(memory_space=pl.ANY), vmem],
        out_specs=(vmem, vmem, vmem),
        scratch_shapes=[
            pltpu.VMEM((512, 4096), BF16),
            pltpu.VMEM((64, 64, 1024), BF16),
            pltpu.VMEM((64, 64, 1024), BF16),
            pltpu.VMEM((512, 1024), F32),
            pltpu.VMEM((512, 1024), F32),
            pltpu.VMEM((512, 2048), BF16),
            pltpu.VMEM((2, 4, 256, 256), BF16),
            pltpu.VMEM((2, 4, 256, 256), BF16),
            pltpu.VMEM((512, 1024), F32),
            pltpu.VMEM((ITERS, 8, 128), F32),
            pltpu.VMEM((ITERS, 3, 8, 128), F32),
            pltpu.VMEM((ITERS, 8, 128), F32),
            pltpu.VMEM((ITERS, 63, 8, 128), F32),
            pltpu.VMEM((2, 8, 128), F32),
            pltpu.VMEM((2, 8, 128), F32),
            dma,
            dma,
            dma,
            dma((4, 49)),
            dma((4, 49)),
            dma((ITERS, 3)),
            dma((ITERS, 3)),
            dma((ITERS,)),
            dma((ITERS,)),
            dma((2,)),
            dma((2,)),
            dma((2, 4)),
            dma((2, 4)),
        ],
        compiler_params=pltpu.CompilerParams(
            collective_id=0, has_side_effects=True, vmem_limit_bytes=58 * 2**20
        ),
        cost_estimate=pl.CostEstimate(flops=18 * 10**9, bytes_accessed=9 * 2**20, transcendentals=3 * 10**6),
    )(noise, data.T)
    return targets, row_pot[:4].reshape(512), col_pot.reshape(1024)


def solution(mesh):
    in_specs = (P("rows", None), P("cols", "rows"))
    out_specs = (P("rows", "cols"), P("rows"), P("cols"))
    return jax.shard_map(
        per_device, mesh=mesh, in_specs=in_specs, out_specs=out_specs, check_vma=False
    )
```

```python
import functools
import math

import jax
import jax.numpy as jnp
from jax import lax
from jax.experimental import pallas as pl
from jax.experimental.pallas import tpu as pltpu
from jax.sharding import PartitionSpec as P

ITERS = 4
EPSILON = 0.05
SCALE_BITS = 64.0
SCALE = 2.0**64
MESH = pl.DeviceIdType.MESH
F32 = jnp.float32
BF16 = jnp.bfloat16


def kernel(
    noise_hbm, data_ref, out_ref, row_ref, col_ref,
    noise_ref, whole_a, whole_b, scores, mass, plan_ref, part_ref, got_ref, own_ref,
    rmsg, rbuf, cmsg, cbuf, pmsg, pbuf,
    nsem, zsend, zrecv, asems, bsems, rsend, rrecv, csend, crecv, psend, precv, tsend, trecv,
):
    rows_total = 32768
    cols_total = 4096
    width = 4096
    to_log2 = 1.0 / (EPSILON * math.log(2.0))
    factor = 2.0 * to_log2 / width
    me = lax.axis_index("rows")
    zh = lax.axis_index("cols")
    y, x, zl, core = me // 16, (me // 4) % 4, (me // 2) % 2, me % 2
    sibling = me + 1 - 2 * core

    def index(yy, xx, ll):
        return ((((yy + 4) % 4) * 4 + (xx + 4) % 4) * 2 + ll) * 2 + core

    load = pltpu.make_async_copy(noise_hbm, noise_ref, nsem)
    load.start()

    barrier = pltpu.get_barrier_semaphore()

    def greet(o, carry):
        pl.semaphore_signal(barrier, inc=1, device_id=((me + o) % 64, zh), device_id_type=MESH)
        return carry

    lax.fori_loop(1, 64, greet, 0)
    for o in range(1, 4):
        pl.semaphore_signal(barrier, inc=1, device_id=(me, (zh + o) % 4), device_id_type=MESH)
    whole_a[me] = data_ref[...]
    pl.semaphore_wait(barrier, 66)

    def place(p, da, db, ll):
        return index(y + db * (1 - p) + da * p, x + da * (1 - p) + db * p, ll)

    def at(p, da, db):
        return place(p, da, db, p)

    def near(p, da, db):
        return place(p, da, db, zl)

    def base(p):
        return 1 + 24 * p

    parts = (zl, 1 - zl)
    turns = (0, -1, 1, 2)

    class Gather:
        def __init__(self, whole, sems):
            self.whole = whole
            self.gsend, self.grecv, self.bsend, self.brecv = sems
            self.sent = []
            self.shared = 0
            self.of_turn = {n: [] for n in range(4)}

        def remote(self, slot, half, send, recv, target):
            ref = self.whole.at[slot] if half is None else self.whole.at[slot, pl.ds(half * 32, 32)]
            return pltpu.make_async_remote_copy(
                src_ref=ref, dst_ref=ref, send_sem=send, recv_sem=recv,
                device_id=(target, zh), device_id_type=MESH,
            )

        def move(self, t, slot, target, half=None):
            copy = self.remote(slot, half, self.gsend.at[t], self.grecv.at[t], target)
            copy.start()
            self.sent.append(copy)

        def arrived(self, t, slot, half=None):
            self.remote(slot, half, self.gsend.at[t], self.grecv.at[t], sibling).wait_recv()

        def share(self, slot, n):
            t = self.shared
            self.shared += 1
            copy = self.remote(slot, None, self.bsend.at[t], self.brecv.at[t], sibling)
            copy.start()
            self.sent.append(copy)
            theirs = slot + 1 - 2 * core
            self.of_turn[n].append(self.remote(theirs, None, self.bsend.at[t], self.brecv.at[t], sibling))

        def launch(self, p):
            self.move(base(p) + 0, at(p, 0, 0), near(p, 1, 0))
            self.move(base(p) + 1, at(p, 0, 0), near(p, -1, 0))
            self.second(0, p)

        def begin(self):
            self.move(0, me, index(y, x, 1 - zl))
            self.launch(zl)
            self.share(me, 0)

        def first(self):
            self.arrived(0, index(y, x, 1 - zl))
            self.launch(1 - zl)
            self.share(index(y, x, 1 - zl), 0)

        def second(self, n, p):
            b = base(p) + 4 + 5 * n
            self.move(b + 0, at(p, turns[n], 0), near(p, 0, 1))
            self.move(b + 1, at(p, turns[n], 0), near(p, 0, -1))

        def turn(self, n, p):
            b = base(p)
            slot = at(p, turns[n], 0)
            if n < 3:
                self.arrived(b + n - 1, slot)
                self.move(b + n + 1, slot, near(p, -turns[n], 0), n - 1)
            else:
                self.arrived(b + 2, slot, 0)
                self.arrived(b + 3, slot, 1)
            self.second(n, p)
            self.share(slot, n)

        def relay(self, n, p):
            b = base(p) + 4 + 5 * n
            for t, db in enumerate((-1, 1)):
                slot = at(p, turns[n], db)
                self.arrived(b + t, slot)
                if t == n % 2:
                    self.move(b + 2, slot, near(p, 0, -db))
                self.share(slot, n)

        def last(self, n):
            for p in parts:
                slot = at(p, turns[n], 2)
                self.arrived(base(p) + 4 + 5 * n + 2, slot)
                self.share(slot, n)

        def turn_done(self, n):
            for copy in self.of_turn[n]:
                copy.wait_recv()

        def done(self):
            for copy in self.sent:
                copy.wait_send()

    def add_gram(whole, scores, n):
        for part in (0, 1):
            firsts = [
                (((i * 4 + (x + turns[n] + 4) % 4) * 2 + part) * 2) if part == 0
                else (((((y + turns[n] + 4) % 4) * 4 + i) * 2 + part) * 2)
                for i in range(4)
            ]
            left = jnp.concatenate(
                [noise_ref[:, pl.ds(pl.multiple_of(f * 64, 128), 128)] for f in firsts], axis=1
            )
            for c in range(4):
                cols = pl.ds(c * 256, 256)
                right = jnp.concatenate(
                    [whole[pl.ds(f, 2), :, cols].reshape(128, 256) for f in firsts], axis=0
                )
                value = factor * jnp.dot(left, right, preferred_element_type=F32)
                scores[:, cols] = value if n == 0 and part == 0 else scores[:, cols] + value

    first_block = Gather(whole_a, [asems.at[i] for i in range(4)])
    other_block = Gather(whole_b, [bsems.at[i] for i in range(4)])

    first_block.begin()
    across = pltpu.make_async_remote_copy(
        src_ref=whole_a.at[me], dst_ref=whole_b.at[me], send_sem=zsend, recv_sem=zrecv,
        device_id=(me, (zh + 2) % 4), device_id_type=MESH,
    )
    first_block.first()
    across.start()
    p, q = parts
    first_block.turn(1, p)
    first_block.turn(1, q)
    first_block.turn(2, p)
    first_block.turn(2, q)
    first_block.relay(0, p)
    first_block.relay(0, q)
    first_block.turn(3, p)
    first_block.turn(3, q)
    first_block.relay(1, p)
    first_block.relay(1, q)
    first_block.relay(2, p)
    first_block.relay(2, q)
    first_block.last(0)
    first_block.relay(3, p)
    first_block.relay(3, q)
    load.wait()
    first_block.turn_done(0)
    add_gram(whole_a, scores, 0)
    across.wait()
    other_block.begin()
    first_block.last(1)
    first_block.turn_done(1)
    add_gram(whole_a, scores, 1)
    other_block.first()
    for n in (2, 3):
        first_block.last(n)
        first_block.turn_done(n)
        add_gram(whole_a, scores, n)

    def square_cols(i, acc):
        v = whole_a[i].astype(F32)
        v = v * v
        return acc + jnp.sum(v.reshape(8, 8, 1024), axis=0)

    data_sq = jnp.sum(lax.fori_loop(0, 64, square_cols, jnp.zeros((8, 1024), F32)), axis=0, keepdims=True)
    diagonal = lax.broadcasted_iota(jnp.int32, (128, 128), 0) == lax.broadcasted_iota(jnp.int32, (128, 128), 1)

    def compact(column):
        parts = [
            jnp.sum(jnp.where(diagonal, column[i * 128:(i + 1) * 128], 0.0), axis=0, keepdims=True)
            for i in range(4)
        ]
        return jnp.concatenate(parts + parts, axis=0)

    def spread(packed):
        parts = [
            jnp.sum(jnp.where(diagonal, packed[i:i + 1], 0.0), axis=1, keepdims=True)
            for i in range(4)
        ]
        return jnp.concatenate(parts, axis=0)

    def fold(line):
        return jnp.concatenate([line[:, i * 128:(i + 1) * 128] for i in range(8)], axis=0)

    def unfold(packed):
        return jnp.concatenate([packed[i:i + 1] for i in range(8)], axis=1)

    def exchange_rows(e, packed, between):
        rmsg[e] = packed
        copies = [
            pltpu.make_async_remote_copy(
                src_ref=rmsg.at[e], dst_ref=rbuf.at[e, o - 1], send_sem=rsend.at[e, o - 1],
                recv_sem=rrecv.at[e, o - 1], device_id=(me, (zh + o) % 4), device_id_type=MESH,
            )
            for o in range(1, 4)
        ]
        for copy in copies:
            copy.start()
        between()
        for copy in copies:
            copy.wait()
        return rbuf[e]

    def exchange_cols(e, packed, between):
        cmsg[e] = packed

        def start(o, carry):
            pltpu.make_async_remote_copy(
                src_ref=cmsg.at[e], dst_ref=cbuf.at[e, o - 1], send_sem=csend.at[e],
                recv_sem=crecv.at[e], device_id=((me + o) % 64, zh), device_id_type=MESH,
            ).start()
            return carry

        lax.fori_loop(1, 64, start, 0)
        between()
        everything = pltpu.make_async_remote_copy(
            src_ref=cbuf.at[e], dst_ref=cbuf.at[e], send_sem=csend.at[e],
            recv_sem=crecv.at[e], device_id=(sibling, zh), device_id_type=MESH,
        )
        everything.wait_recv()
        everything.wait_send()
        return cbuf[e]

    def other_gram(n):
        other_block.last(n)
        other_block.turn_done(n)
        add_gram(whole_b, own_ref, n)

    def step_r1():
        for p in parts:
            other_block.turn(1, p)

    def step_c1():
        for p in parts:
            other_block.turn(2, p)

    def step_r2():
        for p in parts:
            other_block.relay(0, p)
            other_block.turn(3, p)

    def step_c2():
        for p in parts:
            other_block.relay(1, p)

    def step_r3():
        for p in parts:
            other_block.relay(2, p)

    def step_c3():
        for p in parts:
            other_block.relay(3, p)
        other_gram(0)

    def step_r4():
        other_gram(1)

    def step_c4():
        other_gram(2)
        other_gram(3)

    row_steps = (step_r1, step_r2, step_r3, step_r4)
    col_steps = (step_c1, step_c2, step_c3, step_c4)

    def combine(own, others):
        top = jnp.maximum(own, jnp.max(others, axis=0))
        total = jnp.exp2(own - top) + jnp.sum(jnp.exp2(others - top[None]), axis=0)
        return top + jnp.log2(total)

    log_rows = -math.log2(rows_total)
    log_cols = -math.log2(cols_total)

    start_cols = data_sq * (-to_log2 / width)
    logits = scores[...] + start_cols
    top = jnp.max(logits, axis=1, keepdims=True)
    own = compact(top + jnp.log2(jnp.sum(jnp.exp2(logits - top), axis=1, keepdims=True)))
    row_pot = log_rows - combine(own, exchange_rows(0, own, row_steps[0]))
    logits = scores[...] + spread(row_pot)
    top = jnp.max(logits, axis=0, keepdims=True)
    own = fold(top + jnp.log2(jnp.sum(jnp.exp2(logits - top), axis=0, keepdims=True)))
    col_pot = log_cols - combine(own, exchange_cols(0, own, col_steps[0]))
    mass[...] = jnp.exp2(scores[...] + (spread(row_pot) + SCALE_BITS) + unfold(col_pot))

    right_scale = jnp.ones((8, 128), F32)
    for e in range(1, ITERS):
        own = compact(jnp.sum(mass[...] * unfold(right_scale), axis=1, keepdims=True))
        total = own + jnp.sum(exchange_rows(e, own, row_steps[e]), axis=0)
        left_scale = (SCALE / rows_total) / total
        own = fold(jnp.sum(mass[...] * spread(left_scale), axis=0, keepdims=True))
        total = own + jnp.sum(exchange_cols(e, own, col_steps[e]), axis=0)
        right_scale = (SCALE / cols_total) / total

    row_log = row_pot + jnp.log2(left_scale)
    col_log = col_pot + jnp.log2(right_scale)

    pmsg[0] = col_log
    swap = pltpu.make_async_remote_copy(
        src_ref=pmsg.at[0], dst_ref=pbuf.at[0], send_sem=psend.at[0], recv_sem=precv.at[0],
        device_id=(me, (zh + 2) % 4), device_id_type=MESH,
    )
    swap.start()
    row_bits = spread(row_log)
    plan = jnp.exp2(scores[...] + row_bits + unfold(col_log))
    plan_ref[:, :1024] = plan.astype(BF16)
    sums = jnp.sum(plan, axis=1, keepdims=True)

    def product(rows, half, q, c):
        right = (whole_a, whole_b)[half][pl.ds(q * 16 + c * 4, 4)].reshape(256, 1024)
        return lax.dot_general(
            plan_ref[rows, pl.ds(half * 1024, 1024)], right, (((1,), (1,)), ((), ())),
            preferred_element_type=F32,
        )

    sides = ((0, (zh + 1) % 4), (1, (zh + 3) % 4))
    for c in range(4):
        for d, q in sides:
            mass[pl.ds(d * 256, 256), pl.ds(c * 256, 256)] = product(pl.ds(d * 256, 256), 0, q, c)

    swap.wait()
    plan = jnp.exp2(own_ref[...] + row_bits + unfold(pbuf[0]))
    plan_ref[:, 1024:] = plan.astype(BF16)
    sums = sums + jnp.sum(plan, axis=1, keepdims=True)

    hand = []
    for c in range(4):
        for d, q in sides:
            rows = pl.ds(d * 256, 256)
            part_ref[d, c] = (mass[rows, pl.ds(c * 256, 256)] + product(rows, 1, q, c)).astype(BF16)
            copy = pltpu.make_async_remote_copy(
                src_ref=part_ref.at[d, c], dst_ref=got_ref.at[d, c], send_sem=tsend.at[d, c],
                recv_sem=trecv.at[d, c], device_id=(me, q), device_id_type=MESH,
            )
            copy.start()
            hand.append(copy)
    sums = compact(sums)
    pmsg[1] = sums
    tell = pltpu.make_async_remote_copy(
        src_ref=pmsg.at[1], dst_ref=pbuf.at[1], send_sem=psend.at[1], recv_sem=precv.at[1],
        device_id=(me, (zh + 1) % 4), device_id_type=MESH,
    )
    tell.start()
    for c in range(4):
        own_ref[:, pl.ds(c * 256, 256)] = product(pl.ds(0, 512), 0, zh, c) + product(pl.ds(0, 512), 1, zh, c)

    v = noise_ref[...].astype(F32)
    noise_sq = compact(jnp.sum(v * v, axis=1, keepdims=True))
    row_ref[...] = row_log * (1.0 / to_log2) + noise_sq * (1.0 / width)
    col_ref[...] = col_log * (1.0 / to_log2) + fold(data_sq) * (1.0 / width)

    tell.wait()
    inverse = spread(1.0 / (sums + pbuf[1]))
    for c in range(4):
        for d in (0, 1):
            hand[c * 2 + d].wait_recv()
            rows, cols = pl.ds(d * 256, 256), pl.ds(c * 256, 256)
            value = own_ref[rows, cols] + got_ref[d, c].astype(F32)
            out_ref[rows, cols] = (value * inverse[d * 256:(d + 1) * 256]).astype(BF16)
    for copy in hand:
        copy.wait_send()
    first_block.done()
    other_block.done()


def deliver(targets_ref, row_ref, col_ref, targets_out, row_out, col_out):
    targets_out[...] = targets_ref[...]
    for i in range(4):
        row_out[pl.ds(i * 128, 128)] = row_ref[i]
    for i in range(8):
        col_out[pl.ds(i * 128, 128)] = col_ref[i]


def per_device(noise, data):
    vmem = pl.BlockSpec(memory_space=pltpu.VMEM)
    dma = pltpu.SemaphoreType.DMA
    targets, row_pot, col_pot = pl.pallas_call(
        kernel,
        out_shape=(
            jax.ShapeDtypeStruct((512, 1024), BF16),
            jax.ShapeDtypeStruct((8, 128), F32),
            jax.ShapeDtypeStruct((8, 128), F32),
        ),
        in_specs=[pl.BlockSpec(memory_space=pl.ANY), vmem],
        out_specs=(vmem, vmem, vmem),
        scratch_shapes=[
            pltpu.VMEM((512, 4096), BF16),
            pltpu.VMEM((64, 64, 1024), BF16),
            pltpu.VMEM((64, 64, 1024), BF16),
            pltpu.VMEM((512, 1024), F32),
            pltpu.VMEM((512, 1024), F32),
            pltpu.VMEM((512, 2048), BF16),
            pltpu.VMEM((2, 4, 256, 256), BF16),
            pltpu.VMEM((2, 4, 256, 256), BF16),
            pltpu.VMEM((512, 1024), F32),
            pltpu.VMEM((ITERS, 8, 128), F32),
            pltpu.VMEM((ITERS, 3, 8, 128), F32),
            pltpu.VMEM((ITERS, 8, 128), F32),
            pltpu.VMEM((ITERS, 63, 8, 128), F32),
            pltpu.VMEM((2, 8, 128), F32),
            pltpu.VMEM((2, 8, 128), F32),
            dma,
            dma,
            dma,
            dma((4, 49)),
            dma((4, 49)),
            dma((ITERS, 3)),
            dma((ITERS, 3)),
            dma((ITERS,)),
            dma((ITERS,)),
            dma((2,)),
            dma((2,)),
            dma((2, 4)),
            dma((2, 4)),
        ],
        compiler_params=pltpu.CompilerParams(
            collective_id=0, has_side_effects=True, vmem_limit_bytes=58 * 2**20
        ),
        cost_estimate=pl.CostEstimate(flops=18 * 10**9, bytes_accessed=9 * 2**20, transcendentals=3 * 10**6),
    )(noise, data.T)
    return pl.pallas_call(
        deliver,
        out_shape=(
            jax.ShapeDtypeStruct((512, 1024), BF16),
            jax.ShapeDtypeStruct((512,), F32),
            jax.ShapeDtypeStruct((1024,), F32),
        ),
        in_specs=[vmem, vmem, vmem],
        out_specs=(vmem, vmem, vmem),
    )(targets, row_pot, col_pot)


def solution(mesh):
    in_specs = (P("rows", None), P("cols", "rows"))
    out_specs = (P("rows", "cols"), P("rows"), P("cols"))
    return jax.shard_map(
        per_device, mesh=mesh, in_specs=in_specs, out_specs=out_specs, check_vma=False
    )
```

```python
import functools
import math

import jax
import jax.numpy as jnp
from jax import lax
from jax.experimental import pallas as pl
from jax.experimental.pallas import tpu as pltpu
from jax.sharding import PartitionSpec as P

ITERS = 4
EPSILON = 0.05
SCALE_BITS = 64.0
SCALE = 2.0**64
MESH = pl.DeviceIdType.MESH
F32 = jnp.float32
BF16 = jnp.bfloat16


def kernel(
    noise_hbm, data_ref, out_ref, row_ref, col_ref,
    noise_ref, whole_a, whole_b, scores, mass, plan_ref, part_ref, got_ref, own_ref,
    rmsg, rbuf, cmsg, cbuf, pmsg, pbuf,
    news, nsem, zsend, zrecv, asems, bsems, rsend, rrecv, csend, crecv, psend, precv, tsend, trecv,
):
    rows_total = 32768
    cols_total = 4096
    width = 4096
    to_log2 = 1.0 / (EPSILON * math.log(2.0))
    factor = 2.0 * to_log2 / width
    me = lax.axis_index("rows")
    zh = lax.axis_index("cols")
    y, x, zl, core = me // 16, (me // 4) % 4, (me // 2) % 2, me % 2
    sibling = me + 1 - 2 * core

    def index(yy, xx, ll):
        return ((((yy + 4) % 4) * 4 + (xx + 4) % 4) * 2 + ll) * 2 + core

    load = pltpu.make_async_copy(noise_hbm, noise_ref, nsem)
    load.start()

    above = (index(y, x, 1 - zl), lax.rem(zh + zl, 4))
    below = (index(y, x, 1 - zl), lax.rem(zh + 3 + zl, 4))
    barrier = pltpu.get_barrier_semaphore()
    for step in ((1, 0), (-1, 0), (0, 1), (0, -1)):
        beside = (index(y + step[0], x + step[1], zl), zh)
        pl.semaphore_signal(barrier, inc=1, device_id=beside, device_id_type=MESH)
    for beside in (above, below, (sibling, zh)):
        pl.semaphore_signal(barrier, inc=1, device_id=beside, device_id_type=MESH)
    whole_a[me] = data_ref[...]
    pl.semaphore_wait(barrier, 7)

    def place(p, da, db, ll):
        return index(y + db * (1 - p) + da * p, x + da * (1 - p) + db * p, ll)

    def at(p, da, db):
        return place(p, da, db, p)

    def near(p, da, db):
        return place(p, da, db, zl)

    def base(p):
        return 1 + 24 * p

    parts = (zl, 1 - zl)
    turns = (0, -1, 1, 2)

    class Gather:
        def __init__(self, whole, sems):
            self.whole = whole
            self.gsend, self.grecv, self.bsend, self.brecv = sems
            self.sent = []
            self.shared = 0
            self.of_turn = {n: [] for n in range(4)}

        def remote(self, slot, half, send, recv, target):
            ref = self.whole.at[slot] if half is None else self.whole.at[slot, pl.ds(half * 32, 32)]
            return pltpu.make_async_remote_copy(
                src_ref=ref, dst_ref=ref, send_sem=send, recv_sem=recv,
                device_id=(target, zh), device_id_type=MESH,
            )

        def move(self, t, slot, target, half=None):
            copy = self.remote(slot, half, self.gsend.at[t], self.grecv.at[t], target)
            copy.start()
            self.sent.append(copy)

        def arrived(self, t, slot, half=None):
            self.remote(slot, half, self.gsend.at[t], self.grecv.at[t], sibling).wait_recv()

        def share(self, slot, n):
            t = self.shared
            self.shared += 1
            copy = self.remote(slot, None, self.bsend.at[t], self.brecv.at[t], sibling)
            copy.start()
            self.sent.append(copy)
            theirs = slot + 1 - 2 * core
            self.of_turn[n].append(self.remote(theirs, None, self.bsend.at[t], self.brecv.at[t], sibling))

        def launch(self, p):
            self.move(base(p) + 0, at(p, 0, 0), near(p, 1, 0))
            self.move(base(p) + 1, at(p, 0, 0), near(p, -1, 0))
            self.second(0, p)

        def begin(self):
            self.move(0, me, index(y, x, 1 - zl))
            self.launch(zl)
            self.share(me, 0)

        def first(self):
            self.arrived(0, index(y, x, 1 - zl))
            self.launch(1 - zl)
            self.share(index(y, x, 1 - zl), 0)

        def second(self, n, p):
            b = base(p) + 4 + 5 * n
            self.move(b + 0, at(p, turns[n], 0), near(p, 0, 1))
            self.move(b + 1, at(p, turns[n], 0), near(p, 0, -1))

        def turn(self, n, p):
            b = base(p)
            slot = at(p, turns[n], 0)
            if n < 3:
                self.arrived(b + n - 1, slot)
                self.move(b + n + 1, slot, near(p, -turns[n], 0), n - 1)
            else:
                self.arrived(b + 2, slot, 0)
                self.arrived(b + 3, slot, 1)
            self.second(n, p)
            self.share(slot, n)

        def relay(self, n, p):
            b = base(p) + 4 + 5 * n
            for t, db in enumerate((-1, 1)):
                slot = at(p, turns[n], db)
                self.arrived(b + t, slot)
                if t == n % 2:
                    self.move(b + 2, slot, near(p, 0, -db))
                self.share(slot, n)

        def last(self, n):
            for p in parts:
                slot = at(p, turns[n], 2)
                self.arrived(base(p) + 4 + 5 * n + 2, slot)
                self.share(slot, n)

        def turn_done(self, n):
            for copy in self.of_turn[n]:
                copy.wait_recv()

        def done(self):
            for copy in self.sent:
                copy.wait_send()

    def add_gram(whole, scores, n):
        for part in (0, 1):
            firsts = [
                (((i * 4 + (x + turns[n] + 4) % 4) * 2 + part) * 2) if part == 0
                else (((((y + turns[n] + 4) % 4) * 4 + i) * 2 + part) * 2)
                for i in range(4)
            ]
            left = jnp.concatenate(
                [noise_ref[:, pl.ds(pl.multiple_of(f * 64, 128), 128)] for f in firsts], axis=1
            )
            for c in range(4):
                cols = pl.ds(c * 256, 256)
                right = jnp.concatenate(
                    [whole[pl.ds(f, 2), :, cols].reshape(128, 256) for f in firsts], axis=0
                )
                value = factor * jnp.dot(left, right, preferred_element_type=F32)
                scores[:, cols] = value if n == 0 and part == 0 else scores[:, cols] + value

    first_block = Gather(whole_a, [asems.at[i] for i in range(4)])
    other_block = Gather(whole_b, [bsems.at[i] for i in range(4)])

    first_block.begin()
    across = pltpu.make_async_remote_copy(
        src_ref=whole_a.at[me], dst_ref=whole_b.at[me], send_sem=zsend, recv_sem=zrecv,
        device_id=(me, (zh + 2) % 4), device_id_type=MESH,
    )
    pl.semaphore_signal(news.at[0], inc=1, device_id=below, device_id_type=MESH)
    pl.semaphore_signal(news.at[1], inc=1, device_id=above, device_id_type=MESH)
    first_block.first()
    pl.semaphore_wait(news.at[0], 1)
    pl.semaphore_wait(news.at[1], 1)
    pl.semaphore_signal(news.at[2], inc=1, device_id=(me, (zh + 3) % 4), device_id_type=MESH)
    p, q = parts
    first_block.turn(1, p)
    first_block.turn(1, q)
    first_block.turn(2, p)
    first_block.turn(2, q)
    pl.semaphore_wait(news.at[2], 1)
    across.start()
    first_block.relay(0, p)
    first_block.relay(0, q)
    first_block.turn(3, p)
    first_block.turn(3, q)
    first_block.relay(1, p)
    first_block.relay(1, q)
    first_block.relay(2, p)
    first_block.relay(2, q)
    first_block.last(0)
    first_block.relay(3, p)
    first_block.relay(3, q)
    load.wait()
    first_block.turn_done(0)
    add_gram(whole_a, scores, 0)
    across.wait()
    other_block.begin()
    first_block.last(1)
    first_block.turn_done(1)
    add_gram(whole_a, scores, 1)
    other_block.first()
    for n in (2, 3):
        first_block.last(n)
        first_block.turn_done(n)
        add_gram(whole_a, scores, n)

    def square_cols(i, acc):
        v = whole_a[i].astype(F32)
        v = v * v
        return acc + jnp.sum(v.reshape(8, 8, 1024), axis=0)

    data_sq = jnp.sum(lax.fori_loop(0, 64, square_cols, jnp.zeros((8, 1024), F32)), axis=0, keepdims=True)
    diagonal = lax.broadcasted_iota(jnp.int32, (128, 128), 0) == lax.broadcasted_iota(jnp.int32, (128, 128), 1)

    def compact(column):
        parts = [
            jnp.sum(jnp.where(diagonal, column[i * 128:(i + 1) * 128], 0.0), axis=0, keepdims=True)
            for i in range(4)
        ]
        return jnp.concatenate(parts + parts, axis=0)

    def spread(packed):
        parts = [
            jnp.sum(jnp.where(diagonal, packed[i:i + 1], 0.0), axis=1, keepdims=True)
            for i in range(4)
        ]
        return jnp.concatenate(parts, axis=0)

    def fold(line):
        return jnp.concatenate([line[:, i * 128:(i + 1) * 128] for i in range(8)], axis=0)

    def unfold(packed):
        return jnp.concatenate([packed[i:i + 1] for i in range(8)], axis=1)

    def exchange_rows(e, packed, between):
        rmsg[e] = packed
        copies = [
            pltpu.make_async_remote_copy(
                src_ref=rmsg.at[e], dst_ref=rbuf.at[e, o - 1], send_sem=rsend.at[e, o - 1],
                recv_sem=rrecv.at[e, o - 1], device_id=(me, (zh + o) % 4), device_id_type=MESH,
            )
            for o in range(1, 4)
        ]
        for copy in copies:
            copy.start()
        between()
        for copy in copies:
            copy.wait()
        return rbuf[e]

    def exchange_cols(e, packed, between):
        cmsg[e] = packed

        def start(o, carry):
            pltpu.make_async_remote_copy(
                src_ref=cmsg.at[e], dst_ref=cbuf.at[e, o - 1], send_sem=csend.at[e],
                recv_sem=crecv.at[e], device_id=((me + o) % 64, zh), device_id_type=MESH,
            ).start()
            return carry

        lax.fori_loop(1, 64, start, 0)
        between()
        everything = pltpu.make_async_remote_copy(
            src_ref=cbuf.at[e], dst_ref=cbuf.at[e], send_sem=csend.at[e],
            recv_sem=crecv.at[e], device_id=(sibling, zh), device_id_type=MESH,
        )
        everything.wait_recv()
        everything.wait_send()
        return cbuf[e]

    def other_gram(n):
        other_block.last(n)
        other_block.turn_done(n)
        add_gram(whole_b, own_ref, n)

    def step_r1():
        for p in parts:
            other_block.turn(1, p)

    def step_c1():
        for p in parts:
            other_block.turn(2, p)

    def step_r2():
        for p in parts:
            other_block.relay(0, p)
            other_block.turn(3, p)

    def step_c2():
        for p in parts:
            other_block.relay(1, p)

    def step_r3():
        for p in parts:
            other_block.relay(2, p)

    def step_c3():
        for p in parts:
            other_block.relay(3, p)
        other_gram(0)

    def step_r4():
        other_gram(1)

    def step_c4():
        other_gram(2)
        other_gram(3)

    row_steps = (step_r1, step_r2, step_r3, step_r4)
    col_steps = (step_c1, step_c2, step_c3, step_c4)

    def combine(own, others):
        top = jnp.maximum(own, jnp.max(others, axis=0))
        total = jnp.exp2(own - top) + jnp.sum(jnp.exp2(others - top[None]), axis=0)
        return top + jnp.log2(total)

    log_rows = -math.log2(rows_total)
    log_cols = -math.log2(cols_total)

    start_cols = data_sq * (-to_log2 / width)
    logits = scores[...] + start_cols
    top = jnp.max(logits, axis=1, keepdims=True)
    own = compact(top + jnp.log2(jnp.sum(jnp.exp2(logits - top), axis=1, keepdims=True)))
    row_pot = log_rows - combine(own, exchange_rows(0, own, row_steps[0]))
    logits = scores[...] + spread(row_pot)
    top = jnp.max(logits, axis=0, keepdims=True)
    own = fold(top + jnp.log2(jnp.sum(jnp.exp2(logits - top), axis=0, keepdims=True)))
    col_pot = log_cols - combine(own, exchange_cols(0, own, col_steps[0]))
    mass[...] = jnp.exp2(scores[...] + (spread(row_pot) + SCALE_BITS) + unfold(col_pot))

    right_scale = jnp.ones((8, 128), F32)
    for e in range(1, ITERS):
        own = compact(jnp.sum(mass[...] * unfold(right_scale), axis=1, keepdims=True))
        total = own + jnp.sum(exchange_rows(e, own, row_steps[e]), axis=0)
        left_scale = (SCALE / rows_total) / total
        own = fold(jnp.sum(mass[...] * spread(left_scale), axis=0, keepdims=True))
        total = own + jnp.sum(exchange_cols(e, own, col_steps[e]), axis=0)
        right_scale = (SCALE / cols_total) / total

    row_log = row_pot + jnp.log2(left_scale)
    col_log = col_pot + jnp.log2(right_scale)

    pmsg[0] = col_log
    swap = pltpu.make_async_remote_copy(
        src_ref=pmsg.at[0], dst_ref=pbuf.at[0], send_sem=psend.at[0], recv_sem=precv.at[0],
        device_id=(me, (zh + 2) % 4), device_id_type=MESH,
    )
    swap.start()
    row_bits = spread(row_log)
    plan = jnp.exp2(scores[...] + row_bits + unfold(col_log))
    plan_ref[:, :1024] = plan.astype(BF16)
    sums = jnp.sum(plan, axis=1, keepdims=True)

    def product(rows, half, q, c):
        right = (whole_a, whole_b)[half][pl.ds(q * 16 + c * 4, 4)].reshape(256, 1024)
        return lax.dot_general(
            plan_ref[rows, pl.ds(half * 1024, 1024)], right, (((1,), (1,)), ((), ())),
            preferred_element_type=F32,
        )

    sides = ((0, (zh + 1) % 4), (1, (zh + 3) % 4))
    for c in range(4):
        for d, q in sides:
            mass[pl.ds(d * 256, 256), pl.ds(c * 256, 256)] = product(pl.ds(d * 256, 256), 0, q, c)

    swap.wait()
    plan = jnp.exp2(own_ref[...] + row_bits + unfold(pbuf[0]))
    plan_ref[:, 1024:] = plan.astype(BF16)
    sums = sums + jnp.sum(plan, axis=1, keepdims=True)

    hand = []
    for c in range(4):
        for d, q in sides:
            rows = pl.ds(d * 256, 256)
            part_ref[d, c] = (mass[rows, pl.ds(c * 256, 256)] + product(rows, 1, q, c)).astype(BF16)
            copy = pltpu.make_async_remote_copy(
                src_ref=part_ref.at[d, c], dst_ref=got_ref.at[d, c], send_sem=tsend.at[d, c],
                recv_sem=trecv.at[d, c], device_id=(me, q), device_id_type=MESH,
            )
            copy.start()
            hand.append(copy)
    sums = compact(sums)
    pmsg[1] = sums
    tell = pltpu.make_async_remote_copy(
        src_ref=pmsg.at[1], dst_ref=pbuf.at[1], send_sem=psend.at[1], recv_sem=precv.at[1],
        device_id=(me, (zh + 1) % 4), device_id_type=MESH,
    )
    tell.start()
    for c in range(4):
        own_ref[:, pl.ds(c * 256, 256)] = product(pl.ds(0, 512), 0, zh, c) + product(pl.ds(0, 512), 1, zh, c)

    v = noise_ref[...].astype(F32)
    noise_sq = compact(jnp.sum(v * v, axis=1, keepdims=True))
    row_ref[...] = row_log * (1.0 / to_log2) + noise_sq * (1.0 / width)
    col_ref[...] = col_log * (1.0 / to_log2) + fold(data_sq) * (1.0 / width)

    tell.wait()
    inverse = spread(1.0 / (sums + pbuf[1]))
    for c in range(4):
        for d in (0, 1):
            hand[c * 2 + d].wait_recv()
            rows, cols = pl.ds(d * 256, 256), pl.ds(c * 256, 256)
            value = own_ref[rows, cols] + got_ref[d, c].astype(F32)
            out_ref[rows, cols] = (value * inverse[d * 256:(d + 1) * 256]).astype(BF16)
    for copy in hand:
        copy.wait_send()
    first_block.done()
    other_block.done()


def deliver(targets_ref, row_ref, col_ref, targets_out, row_out, col_out):
    targets_out[...] = targets_ref[...]
    for i in range(4):
        row_out[pl.ds(i * 128, 128)] = row_ref[i]
    for i in range(8):
        col_out[pl.ds(i * 128, 128)] = col_ref[i]


def per_device(noise, data):
    vmem = pl.BlockSpec(memory_space=pltpu.VMEM)
    dma = pltpu.SemaphoreType.DMA
    targets, row_pot, col_pot = pl.pallas_call(
        kernel,
        out_shape=(
            jax.ShapeDtypeStruct((512, 1024), BF16),
            jax.ShapeDtypeStruct((8, 128), F32),
            jax.ShapeDtypeStruct((8, 128), F32),
        ),
        in_specs=[pl.BlockSpec(memory_space=pl.ANY), vmem],
        out_specs=(vmem, vmem, vmem),
        scratch_shapes=[
            pltpu.VMEM((512, 4096), BF16),
            pltpu.VMEM((64, 64, 1024), BF16),
            pltpu.VMEM((64, 64, 1024), BF16),
            pltpu.VMEM((512, 1024), F32),
            pltpu.VMEM((512, 1024), F32),
            pltpu.VMEM((512, 2048), BF16),
            pltpu.VMEM((2, 4, 256, 256), BF16),
            pltpu.VMEM((2, 4, 256, 256), BF16),
            pltpu.VMEM((512, 1024), F32),
            pltpu.VMEM((ITERS, 8, 128), F32),
            pltpu.VMEM((ITERS, 3, 8, 128), F32),
            pltpu.VMEM((ITERS, 8, 128), F32),
            pltpu.VMEM((ITERS, 63, 8, 128), F32),
            pltpu.VMEM((2, 8, 128), F32),
            pltpu.VMEM((2, 8, 128), F32),
            pltpu.SemaphoreType.REGULAR((3,)),
            dma,
            dma,
            dma,
            dma((4, 49)),
            dma((4, 49)),
            dma((ITERS, 3)),
            dma((ITERS, 3)),
            dma((ITERS,)),
            dma((ITERS,)),
            dma((2,)),
            dma((2,)),
            dma((2, 4)),
            dma((2, 4)),
        ],
        compiler_params=pltpu.CompilerParams(
            collective_id=0, has_side_effects=True, vmem_limit_bytes=58 * 2**20
        ),
        cost_estimate=pl.CostEstimate(flops=18 * 10**9, bytes_accessed=9 * 2**20, transcendentals=3 * 10**6),
    )(noise, data.T)
    return pl.pallas_call(
        deliver,
        out_shape=(
            jax.ShapeDtypeStruct((512, 1024), BF16),
            jax.ShapeDtypeStruct((512,), F32),
            jax.ShapeDtypeStruct((1024,), F32),
        ),
        in_specs=[vmem, vmem, vmem],
        out_specs=(vmem, vmem, vmem),
    )(targets, row_pot, col_pot)


def solution(mesh):
    in_specs = (P("rows", None), P("cols", "rows"))
    out_specs = (P("rows", "cols"), P("rows"), P("cols"))
    return jax.shard_map(
        per_device, mesh=mesh, in_specs=in_specs, out_specs=out_specs, check_vma=False
    )
```

```python
import functools
import math

import jax
import jax.numpy as jnp
from jax import lax
from jax.experimental import pallas as pl
from jax.experimental.pallas import tpu as pltpu
from jax.sharding import PartitionSpec as P

ITERS = 4
EPSILON = 0.05
SCALE_BITS = 64.0
SCALE = 2.0**64
MESH = pl.DeviceIdType.MESH
F32 = jnp.float32
BF16 = jnp.bfloat16


def kernel(
    noise_hbm, data_ref, out_ref, row_ref, col_ref,
    noise_ref, whole_a, whole_b, scores, mass, plan_ref, part_ref, got_ref, own_ref,
    rmsg, rbuf, cmsg, cbuf, pmsg, pbuf,
    news, nsem, zsend, zrecv, asems, bsems, rsend, rrecv, csend, crecv, psend, precv, tsend, trecv,
):
    rows_total = 32768
    cols_total = 4096
    width = 4096
    to_log2 = 1.0 / (EPSILON * math.log(2.0))
    factor = 2.0 * to_log2 / width
    me = lax.axis_index("rows")
    zh = lax.axis_index("cols")
    y, x, zl, core = me // 16, (me // 4) % 4, (me // 2) % 2, me % 2
    sibling = me + 1 - 2 * core

    def index(yy, xx, ll):
        return ((((yy + 4) % 4) * 4 + (xx + 4) % 4) * 2 + ll) * 2 + core

    load = pltpu.make_async_copy(noise_hbm, noise_ref, nsem)
    load.start()

    above = (index(y, x, 1 - zl), lax.rem(zh + zl, 4))
    below = (index(y, x, 1 - zl), lax.rem(zh + 3 + zl, 4))
    barrier = pltpu.get_barrier_semaphore()
    for step in ((1, 0), (-1, 0), (0, 1), (0, -1)):
        beside = (index(y + step[0], x + step[1], zl), zh)
        pl.semaphore_signal(barrier, inc=1, device_id=beside, device_id_type=MESH)
    for beside in (above, below, (sibling, zh)):
        pl.semaphore_signal(barrier, inc=1, device_id=beside, device_id_type=MESH)
    whole_a[me] = data_ref[...]
    pl.semaphore_wait(barrier, 7)

    def place(p, da, db, ll):
        return index(y + db * (1 - p) + da * p, x + da * (1 - p) + db * p, ll)

    def at(p, da, db):
        return place(p, da, db, p)

    def near(p, da, db):
        return place(p, da, db, zl)

    def base(p):
        return 1 + 24 * p

    parts = (zl, 1 - zl)
    turns = (0, -1, 1, 2)

    class Gather:
        def __init__(self, whole, sems):
            self.whole = whole
            self.gsend, self.grecv, self.bsend, self.brecv = sems
            self.sent = []
            self.shared = 0
            self.of_turn = {n: [] for n in range(4)}

        def remote(self, slot, half, send, recv, target):
            ref = self.whole.at[slot] if half is None else self.whole.at[slot, pl.ds(half * 32, 32)]
            return pltpu.make_async_remote_copy(
                src_ref=ref, dst_ref=ref, send_sem=send, recv_sem=recv,
                device_id=(target, zh), device_id_type=MESH,
            )

        def move(self, t, slot, target, half=None):
            copy = self.remote(slot, half, self.gsend.at[t], self.grecv.at[t], target)
            copy.start()
            self.sent.append(copy)

        def arrived(self, t, slot, half=None):
            self.remote(slot, half, self.gsend.at[t], self.grecv.at[t], sibling).wait_recv()

        def share(self, slot, n):
            t = self.shared
            self.shared += 1
            copy = self.remote(slot, None, self.bsend.at[t], self.brecv.at[t], sibling)
            copy.start()
            self.sent.append(copy)
            theirs = slot + 1 - 2 * core
            self.of_turn[n].append(self.remote(theirs, None, self.bsend.at[t], self.brecv.at[t], sibling))

        def launch(self, p):
            self.move(base(p) + 0, at(p, 0, 0), near(p, 1, 0))
            self.move(base(p) + 1, at(p, 0, 0), near(p, -1, 0))
            self.second(0, p)

        def begin(self):
            self.move(0, me, index(y, x, 1 - zl))
            self.launch(zl)
            self.share(me, 0)

        def first(self):
            self.arrived(0, index(y, x, 1 - zl))
            self.launch(1 - zl)
            self.share(index(y, x, 1 - zl), 0)

        def second(self, n, p):
            b = base(p) + 4 + 5 * n
            self.move(b + 0, at(p, turns[n], 0), near(p, 0, 1))
            self.move(b + 1, at(p, turns[n], 0), near(p, 0, -1))

        def turn(self, n, p):
            b = base(p)
            slot = at(p, turns[n], 0)
            if n < 3:
                self.arrived(b + n - 1, slot)
                self.move(b + n + 1, slot, near(p, -turns[n], 0), n - 1)
            else:
                self.arrived(b + 2, slot, 0)
                self.arrived(b + 3, slot, 1)
            self.second(n, p)
            self.share(slot, n)

        def relay(self, n, p):
            b = base(p) + 4 + 5 * n
            for t, db in enumerate((-1, 1)):
                slot = at(p, turns[n], db)
                self.arrived(b + t, slot)
                if t == n % 2:
                    self.move(b + 2, slot, near(p, 0, -db))
                self.share(slot, n)

        def last(self, n):
            for p in parts:
                slot = at(p, turns[n], 2)
                self.arrived(base(p) + 4 + 5 * n + 2, slot)
                self.share(slot, n)

        def turn_done(self, n):
            for copy in self.of_turn[n]:
                copy.wait_recv()

        def done(self):
            for copy in self.sent:
                copy.wait_send()

    def add_gram(whole, scores, n):
        for part in (0, 1):
            firsts = [
                (((i * 4 + (x + turns[n] + 4) % 4) * 2 + part) * 2) if part == 0
                else (((((y + turns[n] + 4) % 4) * 4 + i) * 2 + part) * 2)
                for i in range(4)
            ]
            left = jnp.concatenate(
                [noise_ref[:, pl.ds(pl.multiple_of(f * 64, 128), 128)] for f in firsts], axis=1
            )
            for c in range(4):
                cols = pl.ds(c * 256, 256)
                right = jnp.concatenate(
                    [whole[pl.ds(f, 2), :, cols].reshape(128, 256) for f in firsts], axis=0
                )
                value = factor * jnp.dot(left, right, preferred_element_type=F32)
                scores[:, cols] = value if n == 0 and part == 0 else scores[:, cols] + value

    first_block = Gather(whole_a, [asems.at[i] for i in range(4)])
    other_block = Gather(whole_b, [bsems.at[i] for i in range(4)])

    first_block.begin()
    across = pltpu.make_async_remote_copy(
        src_ref=whole_a.at[me], dst_ref=whole_b.at[me], send_sem=zsend, recv_sem=zrecv,
        device_id=(me, (zh + 2) % 4), device_id_type=MESH,
    )
    pl.semaphore_signal(news.at[0], inc=1, device_id=below, device_id_type=MESH)
    pl.semaphore_signal(news.at[1], inc=1, device_id=above, device_id_type=MESH)
    first_block.first()
    pl.semaphore_wait(news.at[0], 1)
    pl.semaphore_wait(news.at[1], 1)
    pl.semaphore_signal(news.at[2], inc=1, device_id=(me, (zh + 3) % 4), device_id_type=MESH)
    p, q = parts
    first_block.turn(1, p)
    first_block.turn(1, q)
    first_block.turn(2, p)
    first_block.turn(2, q)
    pl.semaphore_wait(news.at[2], 1)
    across.start()
    first_block.relay(0, p)
    first_block.relay(0, q)
    first_block.turn(3, p)
    first_block.turn(3, q)
    first_block.relay(1, p)
    first_block.relay(1, q)
    first_block.relay(2, p)
    first_block.relay(2, q)
    first_block.last(0)
    first_block.relay(3, p)
    first_block.relay(3, q)
    load.wait()
    first_block.turn_done(0)
    add_gram(whole_a, scores, 0)
    across.wait(); other_block.begin()
    first_block.last(1)
    first_block.turn_done(1)
    add_gram(whole_a, scores, 1)
    other_block.first()
    for n in (2, 3):
        first_block.last(n)
        first_block.turn_done(n)
        add_gram(whole_a, scores, n)

    def square_cols(i, acc):
        v = whole_a[i].astype(F32)
        v = v * v
        return acc + jnp.sum(v.reshape(8, 8, 1024), axis=0)

    data_sq = jnp.sum(lax.fori_loop(0, 64, square_cols, jnp.zeros((8, 1024), F32)), axis=0, keepdims=True)
    diagonal = lax.broadcasted_iota(jnp.int32, (128, 128), 0) == lax.broadcasted_iota(jnp.int32, (128, 128), 1)

    def compact(column):
        parts = [
            jnp.sum(jnp.where(diagonal, column[i * 128:(i + 1) * 128], 0.0), axis=0, keepdims=True)
            for i in range(4)
        ]
        return jnp.concatenate(parts + parts, axis=0)

    def spread(packed):
        parts = [
            jnp.sum(jnp.where(diagonal, packed[i:i + 1], 0.0), axis=1, keepdims=True)
            for i in range(4)
        ]
        return jnp.concatenate(parts, axis=0)

    def fold(line):
        return jnp.concatenate([line[:, i * 128:(i + 1) * 128] for i in range(8)], axis=0)

    def unfold(packed):
        return jnp.concatenate([packed[i:i + 1] for i in range(8)], axis=1)

    def exchange_rows(e, packed, between):
        rmsg[e] = packed
        copies = [
            pltpu.make_async_remote_copy(
                src_ref=rmsg.at[e], dst_ref=rbuf.at[e, o - 1], send_sem=rsend.at[e, o - 1],
                recv_sem=rrecv.at[e, o - 1], device_id=(me, (zh + o) % 4), device_id_type=MESH,
            )
            for o in range(1, 4)
        ]
        for copy in copies:
            copy.start()
        between()
        for copy in copies:
            copy.wait()
        return rbuf[e]

    def exchange_cols(e, packed, between):
        cmsg[e] = packed

        def start(o, carry):
            pltpu.make_async_remote_copy(
                src_ref=cmsg.at[e], dst_ref=cbuf.at[e, o - 1], send_sem=csend.at[e],
                recv_sem=crecv.at[e], device_id=((me + o) % 64, zh), device_id_type=MESH,
            ).start()
            return carry

        lax.fori_loop(1, 64, start, 0)
        between()
        everything = pltpu.make_async_remote_copy(
            src_ref=cbuf.at[e], dst_ref=cbuf.at[e], send_sem=csend.at[e],
            recv_sem=crecv.at[e], device_id=(sibling, zh), device_id_type=MESH,
        )
        everything.wait_recv()
        everything.wait_send()
        return cbuf[e]

    def other_gram(n):
        other_block.last(n)
        other_block.turn_done(n)
        add_gram(whole_b, own_ref, n)

    def step_r1():
        for p in parts:
            other_block.turn(1, p)

    def step_c1():
        for p in parts:
            other_block.turn(2, p)

    def step_r2():
        for p in parts:
            other_block.relay(0, p)

    def step_c2():
        for p in parts:
            other_block.turn(3, p)
        for p in parts:
            other_block.relay(1, p)

    def step_r3():
        for p in parts:
            other_block.relay(2, p)

    def step_c3():
        for p in parts:
            other_block.relay(3, p)
        other_gram(0)

    def step_r4():
        other_gram(1)

    def step_c4():
        other_gram(2)
        other_gram(3)

    row_steps = (step_r1, step_r2, step_r3, step_r4)
    col_steps = (step_c1, step_c2, step_c3, step_c4)

    def combine(own, others):
        top = jnp.maximum(own, jnp.max(others, axis=0))
        total = jnp.exp2(own - top) + jnp.sum(jnp.exp2(others - top[None]), axis=0)
        return top + jnp.log2(total)

    log_rows = -math.log2(rows_total)
    log_cols = -math.log2(cols_total)

    start_cols = data_sq * (-to_log2 / width)
    logits = scores[...] + start_cols
    top = jnp.max(logits, axis=1, keepdims=True)
    own = compact(top + jnp.log2(jnp.sum(jnp.exp2(logits - top), axis=1, keepdims=True)))
    row_pot = log_rows - combine(own, exchange_rows(0, own, row_steps[0]))
    logits = scores[...] + spread(row_pot)
    top = jnp.max(logits, axis=0, keepdims=True)
    own = fold(top + jnp.log2(jnp.sum(jnp.exp2(logits - top), axis=0, keepdims=True)))
    col_pot = log_cols - combine(own, exchange_cols(0, own, col_steps[0]))
    mass[...] = jnp.exp2(scores[...] + (spread(row_pot) + SCALE_BITS) + unfold(col_pot))

    right_scale = jnp.ones((8, 128), F32)
    for e in range(1, ITERS):
        own = compact(jnp.sum(mass[...] * unfold(right_scale), axis=1, keepdims=True))
        total = own + jnp.sum(exchange_rows(e, own, row_steps[e]), axis=0)
        left_scale = (SCALE / rows_total) / total
        own = fold(jnp.sum(mass[...] * spread(left_scale), axis=0, keepdims=True))
        total = own + jnp.sum(exchange_cols(e, own, col_steps[e]), axis=0)
        right_scale = (SCALE / cols_total) / total

    row_log = row_pot + jnp.log2(left_scale)
    col_log = col_pot + jnp.log2(right_scale)

    pmsg[0] = col_log
    swap = pltpu.make_async_remote_copy(
        src_ref=pmsg.at[0], dst_ref=pbuf.at[0], send_sem=psend.at[0], recv_sem=precv.at[0],
        device_id=(me, (zh + 2) % 4), device_id_type=MESH,
    )
    swap.start()
    row_bits = spread(row_log)
    plan = jnp.exp2(scores[...] + row_bits + unfold(col_log))
    plan_ref[:, :1024] = plan.astype(BF16)
    sums = jnp.sum(plan, axis=1, keepdims=True)

    def product(rows, half, q, c):
        right = (whole_a, whole_b)[half][pl.ds(q * 16 + c * 4, 4)].reshape(256, 1024)
        return lax.dot_general(
            plan_ref[rows, pl.ds(half * 1024, 1024)], right, (((1,), (1,)), ((), ())),
            preferred_element_type=F32,
        )

    sides = ((0, (zh + 1) % 4), (1, (zh + 3) % 4))
    for c in range(4):
        for d, q in sides:
            mass[pl.ds(d * 256, 256), pl.ds(c * 256, 256)] = product(pl.ds(d * 256, 256), 0, q, c)

    swap.wait()
    plan = jnp.exp2(own_ref[...] + row_bits + unfold(pbuf[0]))
    plan_ref[:, 1024:] = plan.astype(BF16)
    sums = sums + jnp.sum(plan, axis=1, keepdims=True)

    hand = []
    for c in range(4):
        for d, q in sides:
            rows = pl.ds(d * 256, 256)
            part_ref[d, c] = (mass[rows, pl.ds(c * 256, 256)] + product(rows, 1, q, c)).astype(BF16)
            copy = pltpu.make_async_remote_copy(
                src_ref=part_ref.at[d, c], dst_ref=got_ref.at[d, c], send_sem=tsend.at[d, c],
                recv_sem=trecv.at[d, c], device_id=(me, q), device_id_type=MESH,
            )
            copy.start()
            hand.append(copy)
    sums = compact(sums)
    pmsg[1] = sums
    tell = pltpu.make_async_remote_copy(
        src_ref=pmsg.at[1], dst_ref=pbuf.at[1], send_sem=psend.at[1], recv_sem=precv.at[1],
        device_id=(me, (zh + 1) % 4), device_id_type=MESH,
    )
    tell.start()
    for c in range(4):
        own_ref[:, pl.ds(c * 256, 256)] = product(pl.ds(0, 512), 0, zh, c) + product(pl.ds(0, 512), 1, zh, c)

    v = noise_ref[...].astype(F32)
    noise_sq = compact(jnp.sum(v * v, axis=1, keepdims=True))
    row_ref[...] = row_log * (1.0 / to_log2) + noise_sq * (1.0 / width)
    col_ref[...] = col_log * (1.0 / to_log2) + fold(data_sq) * (1.0 / width)

    tell.wait()
    inverse = spread(1.0 / (sums + pbuf[1]))
    for c in range(4):
        for d in (0, 1):
            hand[c * 2 + d].wait_recv()
            rows, cols = pl.ds(d * 256, 256), pl.ds(c * 256, 256)
            value = own_ref[rows, cols] + got_ref[d, c].astype(F32)
            out_ref[rows, cols] = (value * inverse[d * 256:(d + 1) * 256]).astype(BF16)
    for copy in hand:
        copy.wait_send()
    first_block.done()
    other_block.done()


def deliver(targets_ref, row_ref, col_ref, targets_out, row_out, col_out):
    targets_out[...] = targets_ref[...]
    for i in range(4):
        row_out[pl.ds(i * 128, 128)] = row_ref[i]
    for i in range(8):
        col_out[pl.ds(i * 128, 128)] = col_ref[i]


def per_device(noise, data):
    vmem = pl.BlockSpec(memory_space=pltpu.VMEM)
    dma = pltpu.SemaphoreType.DMA
    targets, row_pot, col_pot = pl.pallas_call(
        kernel,
        out_shape=(
            jax.ShapeDtypeStruct((512, 1024), BF16),
            jax.ShapeDtypeStruct((8, 128), F32),
            jax.ShapeDtypeStruct((8, 128), F32),
        ),
        in_specs=[pl.BlockSpec(memory_space=pl.ANY), vmem],
        out_specs=(vmem, vmem, vmem),
        scratch_shapes=[
            pltpu.VMEM((512, 4096), BF16),
            pltpu.VMEM((64, 64, 1024), BF16),
            pltpu.VMEM((64, 64, 1024), BF16),
            pltpu.VMEM((512, 1024), F32),
            pltpu.VMEM((512, 1024), F32),
            pltpu.VMEM((512, 2048), BF16),
            pltpu.VMEM((2, 4, 256, 256), BF16),
            pltpu.VMEM((2, 4, 256, 256), BF16),
            pltpu.VMEM((512, 1024), F32),
            pltpu.VMEM((ITERS, 8, 128), F32),
            pltpu.VMEM((ITERS, 3, 8, 128), F32),
            pltpu.VMEM((ITERS, 8, 128), F32),
            pltpu.VMEM((ITERS, 63, 8, 128), F32),
            pltpu.VMEM((2, 8, 128), F32),
            pltpu.VMEM((2, 8, 128), F32),
            pltpu.SemaphoreType.REGULAR((3,)),
            dma,
            dma,
            dma,
            dma((4, 49)),
            dma((4, 49)),
            dma((ITERS, 3)),
            dma((ITERS, 3)),
            dma((ITERS,)),
            dma((ITERS,)),
            dma((2,)),
            dma((2,)),
            dma((2, 4)),
            dma((2, 4)),
        ],
        compiler_params=pltpu.CompilerParams(
            collective_id=0, has_side_effects=True, vmem_limit_bytes=58 * 2**20
        ),
        cost_estimate=pl.CostEstimate(flops=18 * 10**9, bytes_accessed=9 * 2**20, transcendentals=3 * 10**6),
    )(noise, data.T)
    return pl.pallas_call(
        deliver,
        out_shape=(
            jax.ShapeDtypeStruct((512, 1024), BF16),
            jax.ShapeDtypeStruct((512,), F32),
            jax.ShapeDtypeStruct((1024,), F32),
        ),
        in_specs=[vmem, vmem, vmem],
        out_specs=(vmem, vmem, vmem),
    )(targets, row_pot, col_pot)


def solution(mesh):
    in_specs = (P("rows", None), P("cols", "rows"))
    out_specs = (P("rows", "cols"), P("rows"), P("cols"))
    return jax.shard_map(
        per_device, mesh=mesh, in_specs=in_specs, out_specs=out_specs, check_vma=False
    )
```
